256 devices in a mesh: orb: 32 (over y, x, core), aux: 8 (over z).
Axes of the slice: x: 4, y: 4, z: 8, core: 2. Of those that a mesh axis runs over, the one named last changes fastest.
Arguments:
- three_centre: bfloat16 [32, 2048, 4096], P('orb', 'aux'), may hold values from -6 to 6
- occ_blocks: bfloat16 [256, 64, 64], P(('orb', 'aux')), may hold values from -0.75 to 0.75
- virt_blocks: bfloat16 [256, 64, 64], P(('orb', 'aux')), may hold values from -0.75 to 0.75
- occ_list: int32 [256], replicated, may hold values from 0 to 255, each once
- virt_list: int32 [256], replicated, may hold values from 0 to 255, each once
- term_count: int32 [32], replicated, may hold values from 1 to 8, 129 in all
Outputs:
- polarizability: float32 [2048, 2048], P('aux', 'orb')
The draws below stay inside these ranges and needn't reach their ends.
Inputs may be any that keep to these rules, and one draw needn't show every extreme that they name: `occ_list`: each slot of the list names one density block; every block is named once. `virt_list`: each slot of the list names one density block; every block is named once. `term_count`: some pair has all 8 terms live.
All inputs are finite; a program needn't handle non-finite values.
Results may differ from the reference program's by a relative error of at most 0.004.
Values may be sent and summed in bfloat16 or wider, within the bound.
No kernel may reach another device: no remote copies, remote signals or barrier semaphores. Data moves between devices by JAX's collectives and lax.ppermute only.
A program may use at most 128 MiB of HBM per device.

```python
import math
import jax
import jax.numpy as jnp
import numpy as np
from jax import lax

BS = 64
NG = 8
PAIRS = 32
AUX = 2048
NDB = 256


def block_levels(own_key, extent, pieces, smallest, largest):
    def one(position, parts):
        heights = jax.random.uniform(jax.random.fold_in(jax.random.fold_in(own_key, 6), position), (parts,), jnp.float32, smallest / len(pieces), largest / len(pieces))
        return jnp.repeat(jnp.exp(heights), extent[position] // parts).reshape((-1,) + (1,) * (len(extent) - position - 1))

    factor_of = one(*pieces[0])
    for cut in pieces[1:]:
        factor_of = factor_of * one(*cut)
    return factor_of


def profile(amount, total, most, skew):
    weights = [(1 << 20) // math.isqrt(rank ** skew) + 1 for rank in range(2, amount + 1)]
    surplus, given = total - most - (amount - 1), [1] * (amount - 1)
    while surplus > 0:
        movable = [i for i in range(amount - 1) if given[i] < most]
        pool, left = sum([weights[i] for i in movable]), surplus
        for i in movable:
            more = min(most - given[i], max(1, left * weights[i] // pool), surplus)
            given[i] = given[i] + more
            surplus = surplus - more
    return np.array([most] + given)


def ragged_sizes(own_key, amount, total, bound, slope):
    if amount == 2:
        one = jax.random.randint(own_key, (), max(1, total - bound), min(bound, total - 1) + 1)
        return jnp.stack([one, total - one])
    tallies = jnp.asarray(profile(amount, total, bound, slope), jnp.int32)
    twos = (amount - 1) // 2
    giver, taker = tallies[1:1 + 2 * twos:2], tallies[2:2 + 2 * twos:2]
    margin = jnp.minimum(giver - 1, bound - taker)
    shifted = jax.random.randint(jax.random.fold_in(own_key, 1), (twos,), 0, 1 << 20) % (margin + 1)
    tallies = tallies.at[1:1 + 2 * twos:2].set(giver - shifted).at[2:2 + 2 * twos:2].set(taker + shifted)
    return tallies[jax.random.permutation(jax.random.fold_in(own_key, 2), amount)]


def normal_values(own_key, extent, spread, bound, shards=(), kind=jnp.bfloat16):
    entries = spread * jax.random.normal(own_key, extent, jnp.float32)
    if shards:
        entries = entries * block_levels(own_key, extent, shards, -0.22, 0.18)
    return jnp.clip(entries, -bound, bound).astype(kind)


def setup_inputs(seed: int = 0) -> dict:
    key_of = jax.random.split(jax.random.key(seed), 7)
    three_centre = normal_values(key_of[0], (PAIRS, AUX, BS * BS), 1.0, 6.0, ((0, 32), (1, 8)))
    occ_blocks = normal_values(key_of[1], (NDB, BS, BS), BS ** -0.5, 0.75, ((0, 256),))
    virt_blocks = normal_values(key_of[2], (NDB, BS, BS), BS ** -0.5, 0.75, ((0, 256),))
    occ_list = jax.random.permutation(key_of[3], NDB).astype(jnp.int32)
    virt_list = jax.random.permutation(key_of[4], NDB).astype(jnp.int32)
    term_count = ragged_sizes(key_of[5], PAIRS, PAIRS * NG // 2 + 1, NG, 2).astype(jnp.int32)
    return dict(three_centre=three_centre, occ_blocks=occ_blocks, virt_blocks=virt_blocks, occ_list=occ_list, virt_list=virt_list, term_count=term_count)


def pair_image(local_block, occ_blocks, virt_blocks, occ_list, virt_list, live_terms, pair_index):
    aux_rows = local_block.shape[0]
    flat_block = local_block.reshape(aux_rows * BS, BS).astype(jnp.float32)

    def add_term(step_index, running):
        live_mask = (step_index < live_terms).astype(jnp.float32)
        list_index = pair_index * NG + step_index
        occ_block = occ_blocks[occ_list[list_index]].astype(jnp.float32)
        virt_block = virt_blocks[virt_list[list_index]].astype(jnp.float32)
        half_image = jnp.dot(flat_block, virt_block).astype(jnp.bfloat16).reshape(aux_rows, BS, BS)
        term_image = jnp.einsum("ml,pms->pls", occ_block, half_image.astype(jnp.float32))
        return running + live_mask * term_image.reshape(aux_rows, BS * BS)

    start_value = jnp.zeros((aux_rows, BS * BS), jnp.float32)
    return lax.fori_loop(0, NG, add_term, start_value).astype(jnp.bfloat16)


def reference(three_centre, occ_blocks, virt_blocks, occ_list, virt_list, term_count):
    summed_chi = jnp.zeros((AUX, AUX), jnp.float32)
    for pair_index in range(PAIRS):
        local_block = three_centre[pair_index]
        image_rows = pair_image(local_block, occ_blocks, virt_blocks, occ_list, virt_list, term_count[pair_index], pair_index)
        summed_chi = summed_chi + lax.dot_general(image_rows, local_block, (((1,), (1,)), ((), ())), preferred_element_type=jnp.float32)
    return summed_chi * (0.25 / BS)
```

```python
import jax
import jax.numpy as jnp
from jax import lax
from jax.experimental import pallas as pl
from jax.experimental.pallas import tpu as pltpu
from jax.sharding import Mesh, PartitionSpec as P

TILES = ((0, 0), (0, 1), (0, -1), (-1, 1), (0, -2), (-1, 2), (2, -1), (2, -2))
B = 64
TERMS = 8
F32, BF16 = jnp.float32, jnp.bfloat16
NT = (((1,), (1,)), ((), ()))


def iota(shape, dim):
    return lax.broadcasted_iota(jnp.int32, shape, dim)


def order_kernel(t_ref, o_ref):
    row, col = iota((256, 256), 0), iota((256, 256), 1)
    source = ((row >> 2) & 3) * 64 + (row >> 4) * 4 + (row & 3)
    pick = jnp.where(source == col, 1.0, 0.0).astype(BF16)
    moved = lax.dot_general(pick, t_ref[...], NT, preferred_element_type=F32)
    o_ref[...] = moved.astype(BF16).reshape(16, 1, 16, 256)


def order_rows(block):
    return pl.pallas_call(
        order_kernel,
        grid=(16,),
        in_specs=[pl.BlockSpec((256, 256), lambda i: (0, i))],
        out_specs=pl.BlockSpec((16, 1, 16, 256), lambda i: (0, i, 0, 0)),
        out_shape=jax.ShapeDtypeStruct((16, 16, 16, 256), BF16),
        cost_estimate=pl.CostEstimate(flops=2 * 16 * 256**3, bytes_accessed=2**22, transcendentals=0),
    )(block)


def weight_kernel(b_ref, w1_ref, w2_ref):
    both = b_ref[0]
    occ, virt = both[:, :B], both[:, B:]
    row, col = iota((256, 256), 0), iota((256, 256), 1)
    tall_row, tall_col = iota((256, B), 0), iota((256, B), 1)
    wide_row, wide_col = iota((B, 256), 0), iota((B, 256), 1)

    def one(hit):
        return jnp.where(hit, 1.0, 0.0).astype(BF16)

    left = one((tall_row >> 4) * 4 + (tall_row & 3) == tall_col)
    right = one((wide_col >> 4) * 4 + (wide_col & 3) == wide_row)
    spread = lax.dot_general(left, virt, NT, preferred_element_type=F32).astype(BF16)
    spread = jnp.dot(spread, right, preferred_element_type=F32)
    w1 = jnp.where(((row >> 2) & 3) == ((col >> 2) & 3), spread, 0.0).astype(BF16)
    w1_ref[...] = w1.reshape(16, 1, 16, 256)

    left = one((tall_row >> 2) == tall_col)
    right = one((wide_col >> 2) == wide_row)
    spread = lax.dot_general(left, occ, NT, preferred_element_type=F32).astype(BF16)
    spread = jnp.dot(spread, right, preferred_element_type=F32)
    w2_ref[...] = jnp.where((row & 3) == (col & 3), spread, 0.0).astype(BF16)


def term_weights(blocks):
    return pl.pallas_call(
        weight_kernel,
        grid=(TERMS,),
        in_specs=[pl.BlockSpec((1, B, 2 * B), lambda j: (j, 0, 0))],
        out_specs=[
            pl.BlockSpec((16, 1, 16, 256), lambda j: (0, j, 0, 0)),
            pl.BlockSpec((256, 256), lambda j: (0, j)),
        ],
        out_shape=[
            jax.ShapeDtypeStruct((16, TERMS, 16, 256), BF16),
            jax.ShapeDtypeStruct((256, TERMS * 256), BF16),
        ],
        cost_estimate=pl.CostEstimate(flops=2**27, bytes_accessed=2**21, transcendentals=0),
    )(blocks)


def image_kernel(t_ref, w1_ref, w2_ref, o_ref, half_ref):
    step = pl.program_id(0)

    @pl.when(step < 16)
    def _():
        slab = t_ref[...].reshape(256, 256)
        for g in range(0, 16, 2):
            part = w1_ref[g:g + 2].reshape(2 * TERMS * 16, 256)
            half = jnp.dot(part, slab, preferred_element_type=F32).astype(BF16)
            half_ref[g:g + 2, :, step] = half.reshape(2, TERMS, 16, 256)

    @pl.when(step >= 16)
    def _():
        half = half_ref[step - 16].reshape(TERMS * 256, 256)
        image = jnp.dot(w2_ref[...], half, preferred_element_type=F32)
        o_ref[...] = image.T.astype(BF16)


def image_rows(block, w1, w2):
    return pl.pallas_call(
        image_kernel,
        grid=(32,),
        in_specs=[
            pl.BlockSpec((16, 1, 16, 256), lambda i: (0, jnp.minimum(i, 15), 0, 0)),
            pl.BlockSpec((16, TERMS, 16, 256), lambda i: (0, 0, 0, 0)),
            pl.BlockSpec((256, TERMS * 256), lambda i: (0, 0)),
        ],
        out_specs=pl.BlockSpec((256, 256), lambda i: (0, jnp.maximum(i - 16, 0))),
        out_shape=jax.ShapeDtypeStruct((256, 4096), BF16),
        scratch_shapes=[pltpu.VMEM((16, TERMS, 16, 16, 256), BF16)],
        compiler_params=pltpu.CompilerParams(vmem_limit_bytes=40 * 2**20),
        cost_estimate=pl.CostEstimate(flops=2 * 256 * 256**3, bytes_accessed=6 * 2**20, transcendentals=0),
    )(block, w1, w2)


def tile_kernel(count, i_ref, *refs):
    step = pl.program_id(0)
    o_ref, sum_ref = refs[count], refs[count + 1]
    image = i_ref[...]
    for n in range(count):
        part = jnp.dot(image, refs[n][...].reshape(1024, 256), preferred_element_type=F32)

        @pl.when(step == 0)
        def _():
            sum_ref[n] = part

        @pl.when(step > 0)
        def _():
            sum_ref[n] += part

        @pl.when(step == 3)
        def _():
            o_ref[n] = sum_ref[n].T


def tiles(image, blocks):
    count = len(blocks)

    def kernel(*refs):
        tile_kernel(count, *refs)

    return pl.pallas_call(
        kernel,
        grid=(4,),
        in_specs=[pl.BlockSpec((256, 1024), lambda i: (0, i))]
        + [pl.BlockSpec((4, 16, 16, 256), lambda i: (i, 0, 0, 0))] * count,
        out_specs=pl.BlockSpec((count, 256, 256), lambda i: (0, 0, 0)),
        out_shape=jax.ShapeDtypeStruct((count, 256, 256), F32),
        scratch_shapes=[pltpu.VMEM((count, 256, 256), F32)],
        compiler_params=pltpu.CompilerParams(vmem_limit_bytes=32 * 2**20),
        cost_estimate=pl.CostEstimate(
            flops=2 * count * 4096 * 256**2, bytes_accessed=(count + 1) * 2**21, transcendentals=0
        ),
    )(image, *blocks)


ALL = ("y", "x", "c", "z")
ORB = ("y", "x", "c")
PLACES = [(y, x, c, z) for y in range(4) for x in range(4) for c in range(2) for z in range(8)]


def number(y, x, c, z):
    return ((y * 4 + x) * 2 + c) * 8 + z


def moved(value, target):
    return lax.ppermute(value, ALL, [(number(*p), number(*target(*p))) for p in PLACES])


def up(value):
    return moved(value, lambda y, x, c, z: (y, x, c, (z + 1) % 8))


def down(value):
    return moved(value, lambda y, x, c, z: (y, x, c, (z + 7) % 8))


def spread_z(block):
    return lax.all_to_all(jnp.broadcast_to(block[None], (8,) + block.shape), "z", 0, 0)


def pair_blocks(occ_block, virt_block, occ_list, virt_list, term_count):
    pair, z = lax.axis_index(ORB), lax.axis_index("z")
    column = spread_z(jnp.concatenate([occ_block, virt_block], axis=1))
    slots = (occ_list.reshape(32, 8), virt_list.reshape(32, 8))
    wanted = [lax.dynamic_index_in_dim(s, z, 1, keepdims=False)[:, None, None] for s in slots]
    wanted = jnp.where(iota((1, 1, 2 * B), 2) < B, wanted[0], wanted[1]) - pair * 8
    outgoing = jnp.zeros((32, B, 2 * B), BF16)
    for r in range(8):
        outgoing = jnp.where(wanted == r, column[r][None], outgoing)
    arrived = lax.all_to_all(outgoing, ORB, 0, 0)
    mine = arrived.astype(F32).sum(0).astype(BF16)
    mine = jnp.where(z < term_count[pair], mine, jnp.zeros_like(mine))
    return spread_z(mine)


def final_place(y, x, c, z):
    row, col = TILES[c * 4 + y]
    orb = ((z + col) % 8) * 4 + x
    return (orb // 8, orb // 2 % 4, orb % 2, (z + row) % 8)


def body(three_centre, occ_blocks, virt_blocks, occ_list, virt_list, term_count):
    held = {0: order_rows(three_centre[0])}
    held[-1], held[1] = up(held[0]), down(held[0])
    held[-2], held[2] = up(held[-1]), down(held[1])
    blocks = pair_blocks(occ_blocks[0], virt_blocks[0], occ_list, virt_list, term_count)
    w1, w2 = term_weights(blocks)
    image = {0: image_rows(held[0], w1, w2)}
    first = tiles(image[0], [held[0], held[1], held[-1]])
    image[-1] = image_rows(held[-1], w1, w2)
    second = tiles(image[-1], [held[1]])
    third = tiles(image[0], [held[-2]])
    fourth = tiles(image[-1], [held[2]])
    image[2] = image_rows(held[2], w1, w2)
    fifth = tiles(image[2], [held[-1], held[-2]])
    core = lax.axis_index("c")
    low = jnp.concatenate([first, second], axis=0)
    high = jnp.concatenate([third, fourth, fifth], axis=0)
    kept, sent = jnp.where(core == 0, low, high), jnp.where(core == 0, high, low)
    total = kept + moved(sent, lambda y, x, c, z: (y, x, 1 - c, z))
    total = lax.all_to_all(total, "y", 0, 0).sum(0)
    total = lax.all_to_all(total.reshape(4, B, 256), "x", 0, 0).sum(0)
    return moved(total * (0.25 / B), final_place).T


def solution(mesh):
    fine = Mesh(mesh.devices.reshape(4, 4, 2, 8), ALL)
    spread = P(ALL, None, None)
    placed = (P(ORB, "z", None), spread, spread, P(), P(), P())
    return jax.shard_map(body, mesh=fine, in_specs=placed, out_specs=P("z", ORB), check_vma=False)
```

```python
import jax
import jax.numpy as jnp
from jax import lax
from jax.experimental import pallas as pl
from jax.experimental.pallas import tpu as pltpu
from jax.sharding import Mesh, PartitionSpec as P

EARLY = ((0, 0, 0), (0, 1, 0), (0, 0, 1), (0, 1, 1), (0, 0, -1), (0, 1, -1), (-1, 1, 1), (1, 0, -1))
LATE = ((-2, 0, 1), (2, 1, -1), (0, 0, 2), (-1, 1, 2), (-2, 0, 2), (0, 1, -2), (1, 0, -2), (2, 1, -2))
B = 64
TERMS = 8
VMEM_LIMIT = 60 * 2**20
F32, BF16 = jnp.float32, jnp.bfloat16
NT = (((1,), (1,)), ((), ()))


def iota(shape, dim):
    return lax.broadcasted_iota(jnp.int32, shape, dim)


def order_kernel(t_ref, a_ref, b_ref):
    row, col = iota((256, 256), 0), iota((256, 256), 1)
    source = ((row >> 2) & 3) * 64 + (row >> 4) * 4 + (row & 3)
    pick = jnp.where(source == col, 1.0, 0.0).astype(BF16)
    for n in range(8):
        piece = t_ref[:, n * 256:(n + 1) * 256]
        turned = lax.dot_general(pick, piece, NT, preferred_element_type=F32).astype(BF16)
        a_ref[:, n] = turned[:, :128].reshape(16, 16, 128)
        b_ref[:, n] = turned[:, 128:].reshape(16, 16, 128)


def order_rows(block):
    half = jax.ShapeDtypeStruct((16, 16, 16, 128), BF16)
    spec = pl.BlockSpec((16, 8, 16, 128), lambda i: (0, i, 0, 0))
    return pl.pallas_call(
        order_kernel,
        grid=(2,),
        in_specs=[pl.BlockSpec((256, 2048), lambda i: (0, i))],
        out_specs=[spec, spec],
        out_shape=[half, half],
        compiler_params=pltpu.CompilerParams(vmem_limit_bytes=VMEM_LIMIT),
        cost_estimate=pl.CostEstimate(flops=2 * 16 * 256**3, bytes_accessed=2**22, transcendentals=0),
    )(block)


def choose_kernel(occ_list, virt_list, c_ref, o_ref):
    y, place = lax.axis_index("y"), lax.axis_index("x") * 2 + lax.axis_index("c")
    left = iota((B, 2 * B), 1) < B

    def one(n, carry):
        occ, virt = occ_list[y * 64 + n], virt_list[y * 64 + n]
        occ_here = (((occ >> 3) & 7) == place).astype(F32)
        virt_here = (((virt >> 3) & 7) == place).astype(F32)
        occ_block = c_ref[(occ >> 6) * 8 + (occ & 7)].astype(F32) * occ_here
        virt_block = c_ref[(virt >> 6) * 8 + (virt & 7)].astype(F32) * virt_here
        o_ref[n] = jnp.where(left, occ_block, virt_block).astype(BF16)
        return carry

    lax.fori_loop(0, 64, one, 0, unroll=8)


SMEM = pl.BlockSpec(memory_space=pltpu.SMEM)


def choose(held, occ_list, virt_list):
    return pl.pallas_call(
        choose_kernel,
        in_specs=[SMEM, SMEM, pl.BlockSpec(memory_space=pltpu.VMEM)],
        out_shape=jax.ShapeDtypeStruct((64, B, 2 * B), BF16),
        cost_estimate=pl.CostEstimate(flops=2**21, bytes_accessed=3 * 2**19, transcendentals=0),
    )(occ_list, virt_list, held)


def weight_kernel(count_ref, b_ref, w1_ref, w2_ref):
    pair = (lax.axis_index("y") * 4 + lax.axis_index("x")) * 2 + lax.axis_index("c")
    live = count_ref[pair]
    row, col = iota((256, 256), 0), iota((256, 256), 1)
    tall_row, tall_col = iota((256, B), 0), iota((256, B), 1)
    wide_row, wide_col = iota((B, 256), 0), iota((B, 256), 1)

    def one(hit):
        return jnp.where(hit, 1.0, 0.0).astype(BF16)

    left_virt = one((tall_row >> 4) * 4 + (tall_row & 3) == tall_col)
    right_virt = one((wide_col >> 4) * 4 + (wide_col & 3) == wide_row)
    keep_virt = ((row >> 2) & 3) == ((col >> 2) & 3)
    left_occ = one((tall_row >> 2) == tall_col)
    right_occ = one((wide_col >> 2) == wide_row)
    keep_occ = (row & 3) == (col & 3)
    for j in range(TERMS):
        both = b_ref[0, j].astype(F32)
        for n in range(1, 8):
            both += b_ref[n, j].astype(F32)
        both = jnp.where(j < live, both, 0.0).astype(BF16)
        occ, virt = both[:, :B], both[:, B:]
        spread = lax.dot_general(left_virt, virt, NT, preferred_element_type=F32).astype(BF16)
        spread = jnp.dot(spread, right_virt, preferred_element_type=F32)
        w1_ref[:, j] = jnp.where(keep_virt, spread, 0.0).astype(BF16).reshape(16, 16, 256)
        spread = lax.dot_general(left_occ, occ, NT, preferred_element_type=F32).astype(BF16)
        spread = jnp.dot(spread, right_occ, preferred_element_type=F32)
        w2_ref[:, j * 256:(j + 1) * 256] = jnp.where(keep_occ, spread, 0.0).astype(BF16)


def term_weights(term_count, blocks):
    return pl.pallas_call(
        weight_kernel,
        in_specs=[SMEM, pl.BlockSpec(memory_space=pltpu.VMEM)],
        out_shape=[
            jax.ShapeDtypeStruct((16, TERMS, 16, 256), BF16),
            jax.ShapeDtypeStruct((256, TERMS * 256), BF16),
        ],
        cost_estimate=pl.CostEstimate(flops=2**28, bytes_accessed=3 * 2**20, transcendentals=0),
    )(term_count, blocks)


def image_kernel(a_ref, b_ref, w1_ref, w2_ref, o_ref, half_ref):
    step = pl.program_id(0)

    @pl.when(step < 2)
    def _():
        for n in range(8):
            slab = jnp.concatenate([a_ref[:, n].reshape(256, 128), b_ref[:, n].reshape(256, 128)], axis=1)
            for g in range(0, 16, 2):
                part = w1_ref[g:g + 2].reshape(2 * TERMS * 16, 256)
                half = jnp.dot(part, slab, preferred_element_type=F32).astype(BF16)
                half_ref[g:g + 2, :, step * 8 + n] = half.reshape(2, TERMS, 16, 256)

    @pl.when(step >= 2)
    def _():
        for n in range(8):
            half = half_ref[(step - 2) * 8 + n].reshape(TERMS * 256, 256)
            image = jnp.dot(w2_ref[...], half, preferred_element_type=F32)
            o_ref[:, n * 256:(n + 1) * 256] = image.T.astype(BF16)


def image_rows(first, second, w1, w2):
    spec = pl.BlockSpec((16, 8, 16, 128), lambda i: (0, jnp.minimum(i, 1), 0, 0))
    return pl.pallas_call(
        image_kernel,
        grid=(4,),
        in_specs=[
            spec,
            spec,
            pl.BlockSpec((16, TERMS, 16, 256), lambda i: (0, 0, 0, 0)),
            pl.BlockSpec((256, TERMS * 256), lambda i: (0, 0)),
        ],
        out_specs=pl.BlockSpec((256, 2048), lambda i: (0, jnp.maximum(i - 2, 0))),
        out_shape=jax.ShapeDtypeStruct((256, 4096), BF16),
        scratch_shapes=[pltpu.VMEM((16, TERMS, 16, 16, 256), BF16)],
        compiler_params=pltpu.CompilerParams(vmem_limit_bytes=VMEM_LIMIT),
        cost_estimate=pl.CostEstimate(flops=2 * 256 * 256**3, bytes_accessed=6 * 2**20, transcendentals=0),
    )(first, second, w1, w2)


def tiles(images, columns, jobs, kind, base=None, given=()):
    count, width = len(images), len(columns)
    rows_of = [len(parts) * 128 for _, parts in jobs]

    def kernel(*refs):
        image_refs, column_refs = refs[:count], refs[count:count + width]
        sums = refs[len(refs) - len(jobs):]
        o_ref = refs[len(refs) - len(jobs) - 1]
        step = pl.program_id(0)
        for (held, parts), sum_ref in zip(jobs, sums):
            block = [column_refs[n][...].reshape(1024, 128) for n, _ in held]
            rows = [image_refs[i][h * 128:(h + 1) * 128] for i, h, _ in parts]
            part = jnp.dot(
                jnp.concatenate(rows, axis=0), jnp.concatenate(block, axis=1), preferred_element_type=F32
            )

            @pl.when(step == 0)
            def _():
                sum_ref[...] = part

            @pl.when(step > 0)
            def _():
                sum_ref[...] += part

        @pl.when(step == 3)
        def _():
            for (held, parts), sum_ref in zip(jobs, sums):
                for r, (_, _, place) in enumerate(parts):
                    for n, (_, side) in enumerate(held):
                        tile = sum_ref[r * 128:(r + 1) * 128, n * 128:(n + 1) * 128].T
                        o_ref[place // 2, 2 * side:2 * side + 2, place % 2] = tile.astype(kind).reshape(2, B, 128)
            for place, side in given:
                at = (place // 2, slice(2 * side, 2 * side + 2), place % 2)
                o_ref[at] = refs[count + width][at]

    whole = pl.BlockSpec((4, 4, 2, B, 128), lambda i: (0, 0, 0, 0, 0))
    flops = sum(2 * 4096 * r * 128 * len(held) for r, (held, _) in zip(rows_of, jobs))
    return pl.pallas_call(
        kernel,
        grid=(4,),
        in_specs=[pl.BlockSpec((256, 1024), lambda i: (0, i))] * count
        + [pl.BlockSpec((4, 16, 16, 128), lambda i: (i, 0, 0, 0))] * width
        + ([] if base is None else [whole]),
        out_specs=whole,
        out_shape=jax.ShapeDtypeStruct((4, 4, 2, B, 128), kind),
        scratch_shapes=[pltpu.VMEM((r, 128 * len(held)), F32) for r, (held, _) in zip(rows_of, jobs)],
        compiler_params=pltpu.CompilerParams(vmem_limit_bytes=VMEM_LIMIT),
        cost_estimate=pl.CostEstimate(
            flops=flops, bytes_accessed=(2 * count + width + 1) * 2**20, transcendentals=0
        ),
    )(*images, *columns, *([] if base is None else [base]))


ALL = ("y", "x", "c", "z")
ORB = ("y", "x", "c")
PLACES = [(y, x, c, z) for y in range(4) for x in range(4) for c in range(2) for z in range(8)]


def number(y, x, c, z):
    return ((y * 4 + x) * 2 + c) * 8 + z


def moved(value, target, places=PLACES):
    return lax.ppermute(value, ALL, [(number(*p), number(*target(*p))) for p in places])


def up(value):
    return moved(value, lambda y, x, c, z: (y, x, c, (z + 1) % 8))


def down(value):
    return moved(value, lambda y, x, c, z: (y, x, c, (z + 7) % 8))


def spread(block, axis, count):
    return lax.all_to_all(jnp.broadcast_to(block[None], (count,) + block.shape), axis, 0, 0)


def along_z(block):
    z = lax.axis_index("z")
    found = [block]
    for n in range(1, 8):
        found.append(moved(block, lambda y, x, c, z: (y, x, c, (z - n) % 8)))
    return jnp.roll(jnp.stack(found), z, axis=0)


def add_up(pieces):
    arrived = lax.all_to_all(pieces.reshape(32, B, 128), ORB, 0, 0)
    return arrived.astype(F32).sum(0) * (0.25 / B)


def placed(total, group):
    def target(y, x, c, z):
        row, _, col = group[y * 2 + c]
        orb = ((z + col) % 8) * 4 + x
        return orb // 8, orb // 2 % 4, orb % 2, (z + row) % 8

    halves = [[p for p in PLACES if group[p[0] * 2 + p[2]][1] == half] for half in range(2)]
    return [moved(total, target, places) for places in halves]


def body(three_centre, occ_blocks, virt_blocks, occ_list, virt_list, term_count):
    both = jnp.concatenate([occ_blocks[0], virt_blocks[0]], axis=1)
    own = order_rows(three_centre[0])
    column = along_z(both)
    own, column = lax.optimization_barrier((own, column))
    below_first, above_first = up(own[0]), down(own[1])
    below_last, above_last = up(own[1]), down(own[0])
    far_below_first, far_above_first = up(below_first), down(above_first)

    held = spread(column, "y", 4).reshape(32, B, 2 * B)
    chosen = choose(held, occ_list, virt_list)
    arrived = lax.all_to_all(chosen.reshape(8, 8, B, 2 * B), ("x", "c"), 0, 0)
    w1, w2 = term_weights(term_count, arrived)
    image = image_rows(own[0], own[1], w1, w2)

    image, below_last, above_last = lax.optimization_barrier((image, below_last, above_last))
    far_below_last, far_above_last = up(below_last), down(above_last)
    near = image_rows(below_last, above_last, w1, w2)
    early = tiles(
        [image, near],
        [own[0], own[1], above_last, above_first, below_first, below_last],
        [
            ([(0, 0), (1, 1)], [(0, 0, 0), (0, 1, 1)]),
            ([(2, 0), (3, 1)], [(0, 0, 2), (0, 1, 3), (1, 0, 6)]),
            ([(4, 0), (5, 1)], [(0, 0, 4), (0, 1, 5), (1, 1, 7)]),
        ],
        F32,
    )
    early, far_below_first, far_above_first = lax.optimization_barrier((early, far_below_first, far_above_first))
    early = add_up(early)
    far = image_rows(far_below_first, far_above_first, w1, w2)
    late_above = [(0, 0, 2), (1, 0, 3), (2, 0, 4)]
    late_below = [(0, 1, 5), (1, 1, 6), (2, 1, 7)]
    late = tiles(
        [image, near, far],
        [above_last, above_first, below_first, below_last, far_above_first, far_below_first],
        [
            ([(0, 0), (1, 1)], [(2, 0, 0)]),
            ([(2, 0), (3, 1)], [(2, 1, 1)]),
            ([(4, 1)], late_above),
            ([(5, 0)], late_below),
        ],
        BF16,
    )
    late, early, far_above_last, far_below_last = lax.optimization_barrier(
        (late, early, far_above_last, far_below_last)
    )
    early = placed(early, EARLY)
    late = tiles(
        [image, near, far],
        [far_above_last, far_below_last],
        [([(0, 0)], late_above), ([(1, 1)], late_below)],
        BF16,
        late,
        [(0, 0), (0, 1), (1, 0), (1, 1), (2, 1), (3, 1), (4, 1), (5, 0), (6, 0), (7, 0)],
    )
    late = placed(add_up(late), LATE)
    return jnp.concatenate([e + l for e, l in zip(early, late)], axis=1).T


def solution(mesh):
    fine = Mesh(mesh.devices.reshape(4, 4, 2, 8), ALL)
    blocks = P(ALL, None, None)
    inputs = (P(ORB, "z", None), blocks, blocks, P(), P(), P())
    return jax.shard_map(body, mesh=fine, in_specs=inputs, out_specs=P("z", ORB), check_vma=False)
```

```python
import jax
import jax.numpy as jnp
from jax import lax
from jax.experimental import pallas as pl
from jax.experimental.pallas import tpu as pltpu
from jax.sharding import Mesh, PartitionSpec as P

TILES = (
    ((0, 0), (0, 0)),
    ((0, 1), (0, 1)),
    ((0, -1), (0, -1)),
    ((0, 2), (-1, 1)),
    ((1, -1), (0, -2)),
    ((-2, 1), (-1, 2)),
    ((1, -2), (2, -1)),
    ((-2, 2), (2, -2)),
)
B = 64
TERMS = 8
VMEM_LIMIT = 60 * 2**20
F32, BF16 = jnp.float32, jnp.bfloat16
NT = (((1,), (1,)), ((), ()))


def iota(shape, dim):
    return lax.broadcasted_iota(jnp.int32, shape, dim)


def order_kernel(t_ref, a_ref, b_ref):
    row, col = iota((256, 256), 0), iota((256, 256), 1)
    source = ((row >> 2) & 3) * 64 + (row >> 4) * 4 + (row & 3)
    pick = jnp.where(source == col, 1.0, 0.0).astype(BF16)
    for n in range(8):
        piece = t_ref[:, n * 256:(n + 1) * 256]
        turned = lax.dot_general(pick, piece, NT, preferred_element_type=F32).astype(BF16)
        a_ref[:, n] = turned[:, :128].reshape(16, 16, 128)
        b_ref[:, n] = turned[:, 128:].reshape(16, 16, 128)


def order_rows(block):
    half = jax.ShapeDtypeStruct((16, 16, 16, 128), BF16)
    spec = pl.BlockSpec((16, 8, 16, 128), lambda i: (0, i, 0, 0))
    return pl.pallas_call(
        order_kernel,
        grid=(2,),
        in_specs=[pl.BlockSpec((256, 2048), lambda i: (0, i))],
        out_specs=[spec, spec],
        out_shape=[half, half],
        compiler_params=pltpu.CompilerParams(vmem_limit_bytes=VMEM_LIMIT),
        cost_estimate=pl.CostEstimate(flops=2 * 16 * 256**3, bytes_accessed=2**22, transcendentals=0),
    )(block)


def choose_kernel(occ_list, virt_list, c_ref, o_ref):
    y, place = lax.axis_index("y"), lax.axis_index("x") * 2 + lax.axis_index("c")
    left = iota((B, 2 * B), 1) < B

    def one(n, carry):
        occ, virt = occ_list[y * 64 + n], virt_list[y * 64 + n]
        occ_here = (((occ >> 3) & 7) == place).astype(F32)
        virt_here = (((virt >> 3) & 7) == place).astype(F32)
        occ_block = c_ref[(occ >> 6) * 8 + (occ & 7)].astype(F32) * occ_here
        virt_block = c_ref[(virt >> 6) * 8 + (virt & 7)].astype(F32) * virt_here
        o_ref[n] = jnp.where(left, occ_block, virt_block).astype(BF16)
        return carry

    lax.fori_loop(0, 64, one, 0, unroll=8)


SMEM = pl.BlockSpec(memory_space=pltpu.SMEM)


def choose(held, occ_list, virt_list):
    return pl.pallas_call(
        choose_kernel,
        in_specs=[SMEM, SMEM, pl.BlockSpec(memory_space=pltpu.VMEM)],
        out_shape=jax.ShapeDtypeStruct((64, B, 2 * B), BF16),
        cost_estimate=pl.CostEstimate(flops=120 * 256**3, bytes_accessed=3 * 2**19, transcendentals=0),
    )(occ_list, virt_list, held)


def weight_kernel(count_ref, b_ref, w1_ref, w2_ref):
    pair = (lax.axis_index("y") * 4 + lax.axis_index("x")) * 2 + lax.axis_index("c")
    live = count_ref[pair]
    row, col = iota((256, 256), 0), iota((256, 256), 1)
    tall_row, tall_col = iota((256, B), 0), iota((256, B), 1)
    wide_row, wide_col = iota((B, 256), 0), iota((B, 256), 1)

    def one(hit):
        return jnp.where(hit, 1.0, 0.0).astype(BF16)

    left_virt = one((tall_row >> 4) * 4 + (tall_row & 3) == tall_col)
    right_virt = one((wide_col >> 4) * 4 + (wide_col & 3) == wide_row)
    keep_virt = ((row >> 2) & 3) == ((col >> 2) & 3)
    left_occ = one((tall_row >> 2) == tall_col)
    right_occ = one((wide_col >> 2) == wide_row)
    keep_occ = (row & 3) == (col & 3)
    for j in range(TERMS):
        both = b_ref[0, j].astype(F32)
        for n in range(1, 8):
            both += b_ref[n, j].astype(F32)
        both = jnp.where(j < live, both, 0.0).astype(BF16)
        occ, virt = both[:, :B], both[:, B:]
        spread = lax.dot_general(left_virt, virt, NT, preferred_element_type=F32).astype(BF16)
        spread = jnp.dot(spread, right_virt, preferred_element_type=F32)
        w1_ref[:, j] = jnp.where(keep_virt, spread, 0.0).astype(BF16).reshape(16, 16, 256)
        spread = lax.dot_general(left_occ, occ, NT, preferred_element_type=F32).astype(BF16)
        spread = jnp.dot(spread, right_occ, preferred_element_type=F32)
        w2_ref[:, j * 256:(j + 1) * 256] = jnp.where(keep_occ, spread, 0.0).astype(BF16)


def term_weights(term_count, blocks):
    return pl.pallas_call(
        weight_kernel,
        in_specs=[SMEM, pl.BlockSpec(memory_space=pltpu.VMEM)],
        out_shape=[
            jax.ShapeDtypeStruct((16, TERMS, 16, 256), BF16),
            jax.ShapeDtypeStruct((256, TERMS * 256), BF16),
        ],
        cost_estimate=pl.CostEstimate(flops=200 * 256**3, bytes_accessed=3 * 2**20, transcendentals=0),
    )(term_count, blocks)


def image_kernel(a_ref, b_ref, w1_ref, w2_ref, o_ref, half_ref):
    step = pl.program_id(0)

    @pl.when(step < 2)
    def _():
        for n in range(8):
            slab = jnp.concatenate([a_ref[:, n].reshape(256, 128), b_ref[:, n].reshape(256, 128)], axis=1)
            for g in range(0, 16, 2):
                part = w1_ref[g:g + 2].reshape(2 * TERMS * 16, 256)
                half = jnp.dot(part, slab, preferred_element_type=F32).astype(BF16)
                half_ref[g:g + 2, :, step * 8 + n] = half.reshape(2, TERMS, 16, 256)

    @pl.when(step >= 2)
    def _():
        for n in range(8):
            half = half_ref[(step - 2) * 8 + n].reshape(TERMS * 256, 256)
            image = jnp.dot(w2_ref[...], half, preferred_element_type=F32)
            o_ref[:, n * 256:(n + 1) * 256] = image.T.astype(BF16)


def image_rows(first, second, w1, w2):
    spec = pl.BlockSpec((16, 8, 16, 128), lambda i: (0, jnp.minimum(i, 1), 0, 0))
    return pl.pallas_call(
        image_kernel,
        grid=(4,),
        in_specs=[
            spec,
            spec,
            pl.BlockSpec((16, TERMS, 16, 256), lambda i: (0, 0, 0, 0)),
            pl.BlockSpec((256, TERMS * 256), lambda i: (0, 0)),
        ],
        out_specs=pl.BlockSpec((256, 2048), lambda i: (0, jnp.maximum(i - 2, 0))),
        out_shape=jax.ShapeDtypeStruct((256, 4096), BF16),
        scratch_shapes=[pltpu.VMEM((16, TERMS, 16, 16, 256), BF16)],
        compiler_params=pltpu.CompilerParams(vmem_limit_bytes=VMEM_LIMIT),
        cost_estimate=pl.CostEstimate(flops=512 * 256**3, bytes_accessed=6 * 2**20, transcendentals=0),
    )(first, second, w1, w2)


def tiles(images, columns, jobs, base=None, given=()):
    count, width = len(images), len(columns)
    rows_of = [len(parts) * 128 for _, parts in jobs]

    def at(place, side):
        tile, half = place
        return tile // 2, slice(2 * side, 2 * side + 2), tile % 2, slice(half * B, (half + 1) * B)

    def kernel(*refs):
        image_refs, column_refs = refs[:count], refs[count:count + width]
        sums = refs[len(refs) - len(jobs):]
        o_ref = refs[len(refs) - len(jobs) - 1]
        step = pl.program_id(0)
        for (held, parts), sum_ref in zip(jobs, sums):
            block = [column_refs[n][...].reshape(1024, 128) for n, _ in held]
            rows = [image_refs[i][h * 128:(h + 1) * 128] for i, h, _ in parts]
            part = jnp.dot(
                jnp.concatenate(rows, axis=0), jnp.concatenate(block, axis=1), preferred_element_type=F32
            )
            sum_ref[...] = jnp.where(step == 0, 0.0, sum_ref[...]) + part

        @pl.when(step == 3)
        def _():
            for (held, parts), sum_ref in zip(jobs, sums):
                for r, (_, _, place) in enumerate(parts):
                    for n, (_, side) in enumerate(held):
                        tile = sum_ref[r * 128:(r + 1) * 128, n * 128:(n + 1) * 128].T
                        o_ref[at(place, side)] = tile.astype(BF16).reshape(2, B, 128)
            for place, side in given:
                o_ref[at(place, side)] = refs[count + width][at(place, side)]

    whole = pl.BlockSpec((4, 4, 2, 2 * B, 128), lambda i: (0, 0, 0, 0, 0))
    flops = sum(2 * 4096 * r * 128 * len(held) for r, (held, _) in zip(rows_of, jobs))
    return pl.pallas_call(
        kernel,
        grid=(4,),
        in_specs=[pl.BlockSpec((256, 1024), lambda i: (0, i))] * count
        + [pl.BlockSpec((4, 16, 16, 128), lambda i: (i, 0, 0, 0))] * width
        + ([] if base is None else [whole]),
        out_specs=whole,
        out_shape=jax.ShapeDtypeStruct((4, 4, 2, 2 * B, 128), BF16),
        scratch_shapes=[pltpu.VMEM((r, 128 * len(held)), F32) for r, (held, _) in zip(rows_of, jobs)],
        compiler_params=pltpu.CompilerParams(vmem_limit_bytes=VMEM_LIMIT),
        cost_estimate=pl.CostEstimate(
            flops=flops, bytes_accessed=(2 * count + width + 2) * 2**20, transcendentals=0
        ),
    )(*images, *columns, *([] if base is None else [base]))


ALL = ("y", "x", "c", "z")
ORB = ("y", "x", "c")
PLACES = [(y, x, c, z) for y in range(4) for x in range(4) for c in range(2) for z in range(8)]


def number(y, x, c, z):
    return ((y * 4 + x) * 2 + c) * 8 + z


def moved(value, target, places=PLACES):
    return lax.ppermute(value, ALL, [(number(*p), number(*target(*p))) for p in places])


def up(value):
    return moved(value, lambda y, x, c, z: (y, x, c, (z + 1) % 8))


def down(value):
    return moved(value, lambda y, x, c, z: (y, x, c, (z + 7) % 8))


def spread(block, axis, count):
    return lax.all_to_all(jnp.broadcast_to(block[None], (count,) + block.shape), axis, 0, 0)


def add_up(pieces):
    arrived = lax.all_to_all(pieces.reshape(32, 2 * B, 128), ORB, 0, 0)
    total = arrived.astype(F32).sum(0) * (0.25 / B)

    def send(half):
        def target(y, x, c, z):
            row, col = TILES[y * 2 + c][half]
            orb = ((z + col) % 8) * 4 + x
            return orb // 8, orb // 2 % 4, orb % 2, (z + row) % 8

        return moved(total[half * B:(half + 1) * B], target)

    return jnp.concatenate([send(0), send(1)], axis=1).T


def body(three_centre, occ_blocks, virt_blocks, occ_list, virt_list, term_count):
    both = jnp.concatenate([occ_blocks[0], virt_blocks[0]], axis=1)
    own = order_rows(three_centre[0])
    column = spread(both, "z", 8)
    below_first, above_first = up(own[0]), down(own[1])
    below_last, above_last = up(own[1]), down(own[0])
    far_below_first, far_above_first = up(below_first), down(above_first)

    held = spread(column, "y", 4).reshape(32, B, 2 * B)
    chosen = choose(held, occ_list, virt_list)
    arrived = lax.all_to_all(chosen.reshape(8, 8, B, 2 * B), ("x", "c"), 0, 0)
    w1, w2 = term_weights(term_count, arrived)
    image = image_rows(own[0], own[1], w1, w2)

    image, below_last, above_last = lax.optimization_barrier((image, below_last, above_last))
    far_below_last, far_above_last = up(below_last), down(above_last)
    near = image_rows(below_last, above_last, w1, w2)
    above, below = [(2, 0), (3, 1)], [(4, 0), (5, 1)]
    columns = [own[0], own[1], above_last, above_first, below_first, below_last]
    sums = tiles(
        [image, near],
        columns,
        [
            ([(0, 0), (1, 1)], [(0, 0, (0, 0)), (0, 1, (0, 1))]),
            (above, [(0, 0, (1, 0)), (0, 1, (1, 1)), (1, 0, (3, 1))]),
            (below, [(0, 0, (2, 0)), (0, 1, (2, 1)), (1, 1, (4, 0))]),
        ],
    )
    early = [(0, 0), (0, 1), (1, 0), (1, 1), (3, 1), (2, 0), (2, 1), (4, 0)]
    given = [(place, side) for place in early for side in range(2)]
    sums, far_below_first, far_above_first = lax.optimization_barrier((sums, far_below_first, far_above_first))
    far = image_rows(far_below_first, far_above_first, w1, w2)
    far_above = [(0, 0, (3, 0)), (1, 0, (5, 1)), (2, 0, (7, 0))]
    far_below = [(0, 1, (4, 1)), (1, 1, (6, 0)), (2, 1, (7, 1))]
    sums = tiles(
        [image, near, far],
        columns[2:] + [far_above_first, far_below_first],
        [
            ([(0, 0), (1, 1)], [(2, 0, (5, 0))]),
            ([(2, 0), (3, 1)], [(2, 1, (6, 1))]),
            ([(4, 1)], far_above),
            ([(5, 0)], far_below),
        ],
        sums,
        given,
    )
    given = given + [((5, 0), 0), ((5, 0), 1), ((6, 1), 0), ((6, 1), 1)]
    given = given + [(place, 1) for _, _, place in far_above] + [(place, 0) for _, _, place in far_below]
    sums, far_above_last, far_below_last = lax.optimization_barrier((sums, far_above_last, far_below_last))
    sums = tiles(
        [image, near, far],
        [far_above_last, far_below_last],
        [([(0, 0)], far_above), ([(1, 1)], far_below)],
        sums,
        given,
    )
    return add_up(sums)


def solution(mesh):
    fine = Mesh(mesh.devices.reshape(4, 4, 2, 8), ALL)
    blocks = P(ALL, None, None)
    inputs = (P(ORB, "z", None), blocks, blocks, P(), P(), P())
    return jax.shard_map(body, mesh=fine, in_specs=inputs, out_specs=P("z", ORB), check_vma=False)
```

```python
import jax
import jax.numpy as jnp
from jax import lax
from jax.experimental import pallas as pl
from jax.experimental.pallas import tpu as pltpu
from jax.sharding import Mesh, PartitionSpec as P

TILES = (
    ((0, 0), (0, 0)),
    ((0, 1), (0, 1)),
    ((0, -1), (0, -1)),
    ((0, 2), (-1, 1)),
    ((1, -1), (0, -2)),
    ((-2, 1), (-1, 2)),
    ((1, -2), (2, -1)),
    ((-2, 2), (2, -2)),
)
B = 64
TERMS = 8
VMEM_LIMIT = 60 * 2**20
F32, BF16 = jnp.float32, jnp.bfloat16
NT = (((1,), (1,)), ((), ()))


def iota(shape, dim):
    return lax.broadcasted_iota(jnp.int32, shape, dim)


def order_kernel(t_ref, a_ref, b_ref):
    row, col = iota((256, 256), 0), iota((256, 256), 1)
    source = ((row >> 2) & 3) * 64 + (row >> 4) * 4 + (row & 3)
    pick = jnp.where(source == col, 1.0, 0.0).astype(BF16)
    for n in range(8):
        piece = t_ref[:, n * 256:(n + 1) * 256]
        turned = lax.dot_general(pick, piece, NT, preferred_element_type=F32).astype(BF16)
        a_ref[:, n] = turned[:, :128].reshape(16, 16, 128)
        b_ref[:, n] = turned[:, 128:].reshape(16, 16, 128)


def order_rows(block):
    half = jax.ShapeDtypeStruct((16, 16, 16, 128), BF16)
    spec = pl.BlockSpec((16, 8, 16, 128), lambda i: (0, i, 0, 0))
    return pl.pallas_call(
        order_kernel,
        grid=(2,),
        in_specs=[pl.BlockSpec((256, 2048), lambda i: (0, i))],
        out_specs=[spec, spec],
        out_shape=[half, half],
        compiler_params=pltpu.CompilerParams(vmem_limit_bytes=VMEM_LIMIT),
        cost_estimate=pl.CostEstimate(flops=2 * 16 * 256**3, bytes_accessed=2**22, transcendentals=0),
    )(block)


def choose_kernel(occ_list, virt_list, c_ref, o_ref):
    y, place = lax.axis_index("y"), lax.axis_index("x") * 2 + lax.axis_index("c")
    left = iota((B, 2 * B), 1) < B

    def one(n, carry):
        occ, virt = occ_list[y * 64 + n], virt_list[y * 64 + n]
        occ_here = (((occ >> 3) & 7) == place).astype(F32)
        virt_here = (((virt >> 3) & 7) == place).astype(F32)
        occ_block = c_ref[((y - (occ >> 6)) & 3) * 8 + (occ & 7)].astype(F32) * occ_here
        virt_block = c_ref[((y - (virt >> 6)) & 3) * 8 + (virt & 7)].astype(F32) * virt_here
        o_ref[n] = jnp.where(left, occ_block, virt_block).astype(BF16)
        return carry

    lax.fori_loop(0, 64, one, 0, unroll=8)


SMEM = pl.BlockSpec(memory_space=pltpu.SMEM)


def choose(held, occ_list, virt_list):
    return pl.pallas_call(
        choose_kernel,
        in_specs=[SMEM, SMEM, pl.BlockSpec(memory_space=pltpu.VMEM)],
        out_shape=jax.ShapeDtypeStruct((64, B, 2 * B), BF16),
        cost_estimate=pl.CostEstimate(flops=120 * 256**3, bytes_accessed=3 * 2**19, transcendentals=0),
    )(occ_list, virt_list, held)


def weight_kernel(count_ref, b_ref, w1_ref, w2_ref):
    pair = (lax.axis_index("y") * 4 + lax.axis_index("x")) * 2 + lax.axis_index("c")
    live = count_ref[pair]
    row, col = iota((256, 256), 0), iota((256, 256), 1)
    tall_row, tall_col = iota((256, B), 0), iota((256, B), 1)
    wide_row, wide_col = iota((B, 256), 0), iota((B, 256), 1)

    def one(hit):
        return jnp.where(hit, 1.0, 0.0).astype(BF16)

    left_virt = one((tall_row >> 4) * 4 + (tall_row & 3) == tall_col)
    right_virt = one((wide_col >> 4) * 4 + (wide_col & 3) == wide_row)
    keep_virt = ((row >> 2) & 3) == ((col >> 2) & 3)
    left_occ = one((tall_row >> 2) == tall_col)
    right_occ = one((wide_col >> 2) == wide_row)
    keep_occ = (row & 3) == (col & 3)
    for j in range(TERMS):
        both = b_ref[0, j].astype(F32)
        for n in range(1, 8):
            both += b_ref[n, j].astype(F32)
        both = jnp.where(j < live, both, 0.0).astype(BF16)
        occ, virt = both[:, :B], both[:, B:]
        spread = lax.dot_general(left_virt, virt, NT, preferred_element_type=F32).astype(BF16)
        spread = jnp.dot(spread, right_virt, preferred_element_type=F32)
        w1_ref[:, j] = jnp.where(keep_virt, spread, 0.0).astype(BF16).reshape(16, 16, 256)
        spread = lax.dot_general(left_occ, occ, NT, preferred_element_type=F32).astype(BF16)
        spread = jnp.dot(spread, right_occ, preferred_element_type=F32)
        w2_ref[:, j * 256:(j + 1) * 256] = jnp.where(keep_occ, spread, 0.0).astype(BF16)


def term_weights(term_count, blocks):
    return pl.pallas_call(
        weight_kernel,
        in_specs=[SMEM, pl.BlockSpec(memory_space=pltpu.VMEM)],
        out_shape=[
            jax.ShapeDtypeStruct((16, TERMS, 16, 256), BF16),
            jax.ShapeDtypeStruct((256, TERMS * 256), BF16),
        ],
        cost_estimate=pl.CostEstimate(flops=200 * 256**3, bytes_accessed=3 * 2**20, transcendentals=0),
    )(term_count, blocks)


def image_kernel(a_ref, b_ref, w1_ref, w2_ref, o_ref, half_ref):
    step = pl.program_id(0)

    @pl.when(step < 2)
    def _():
        for n in range(8):
            slab = jnp.concatenate([a_ref[:, n].reshape(256, 128), b_ref[:, n].reshape(256, 128)], axis=1)
            for g in range(0, 16, 2):
                part = w1_ref[g:g + 2].reshape(2 * TERMS * 16, 256)
                half = jnp.dot(part, slab, preferred_element_type=F32).astype(BF16)
                half_ref[g:g + 2, :, step * 8 + n] = half.reshape(2, TERMS, 16, 256)

    @pl.when(step >= 2)
    def _():
        for n in range(8):
            half = half_ref[(step - 2) * 8 + n].reshape(TERMS * 256, 256)
            image = jnp.dot(w2_ref[...], half, preferred_element_type=F32)
            o_ref[:, n * 256:(n + 1) * 256] = image.T.astype(BF16)


def image_rows(first, second, w1, w2):
    spec = pl.BlockSpec((16, 8, 16, 128), lambda i: (0, jnp.minimum(i, 1), 0, 0))
    return pl.pallas_call(
        image_kernel,
        grid=(4,),
        in_specs=[
            spec,
            spec,
            pl.BlockSpec((16, TERMS, 16, 256), lambda i: (0, 0, 0, 0)),
            pl.BlockSpec((256, TERMS * 256), lambda i: (0, 0)),
        ],
        out_specs=pl.BlockSpec((256, 2048), lambda i: (0, jnp.maximum(i - 2, 0))),
        out_shape=jax.ShapeDtypeStruct((256, 4096), BF16),
        scratch_shapes=[pltpu.VMEM((16, TERMS, 16, 16, 256), BF16)],
        compiler_params=pltpu.CompilerParams(vmem_limit_bytes=VMEM_LIMIT),
        cost_estimate=pl.CostEstimate(flops=512 * 256**3, bytes_accessed=6 * 2**20, transcendentals=0),
    )(first, second, w1, w2)


def tiles(images, columns, jobs, base=None, given=()):
    count, width = len(images), len(columns)
    rows_of = [len(parts) * 128 for _, parts in jobs]

    def at(place, side):
        tile, half = place
        return tile // 2, slice(2 * side, 2 * side + 2), tile % 2, slice(half * B, (half + 1) * B)

    def kernel(*refs):
        image_refs, column_refs = refs[:count], refs[count:count + width]
        sums = refs[len(refs) - len(jobs):]
        o_ref = refs[len(refs) - len(jobs) - 1]
        step = pl.program_id(0)
        for (held, parts), sum_ref in zip(jobs, sums):
            block = [column_refs[n][...].reshape(1024, 128) for n, _ in held]
            rows = [image_refs[i][h * 128:(h + 1) * 128] for i, h, _ in parts]
            part = jnp.dot(
                jnp.concatenate(rows, axis=0), jnp.concatenate(block, axis=1), preferred_element_type=F32
            )
            sum_ref[...] = jnp.where(step == 0, 0.0, sum_ref[...]) + part

        @pl.when(step == 3)
        def _():
            for (held, parts), sum_ref in zip(jobs, sums):
                for r, (_, _, place) in enumerate(parts):
                    for n, (_, side) in enumerate(held):
                        tile = sum_ref[r * 128:(r + 1) * 128, n * 128:(n + 1) * 128].T
                        o_ref[at(place, side)] = tile.astype(BF16).reshape(2, B, 128)
            for place, side in given:
                o_ref[at(place, side)] = refs[count + width][at(place, side)]

    whole = pl.BlockSpec((4, 4, 2, 2 * B, 128), lambda i: (0, 0, 0, 0, 0))
    flops = sum(2 * 4096 * r * 128 * len(held) for r, (held, _) in zip(rows_of, jobs))
    return pl.pallas_call(
        kernel,
        grid=(4,),
        in_specs=[pl.BlockSpec((256, 1024), lambda i: (0, i))] * count
        + [pl.BlockSpec((4, 16, 16, 128), lambda i: (i, 0, 0, 0))] * width
        + ([] if base is None else [whole]),
        out_specs=whole,
        out_shape=jax.ShapeDtypeStruct((4, 4, 2, 2 * B, 128), BF16),
        scratch_shapes=[pltpu.VMEM((r, 128 * len(held)), F32) for r, (held, _) in zip(rows_of, jobs)],
        compiler_params=pltpu.CompilerParams(vmem_limit_bytes=VMEM_LIMIT),
        cost_estimate=pl.CostEstimate(
            flops=flops, bytes_accessed=(2 * count + width + 2) * 2**20, transcendentals=0
        ),
    )(*images, *columns, *([] if base is None else [base]))


ALL = ("y", "x", "c", "z")
ORB = ("y", "x", "c")
PLACES = [(y, x, c, z) for y in range(4) for x in range(4) for c in range(2) for z in range(8)]


def number(y, x, c, z):
    return ((y * 4 + x) * 2 + c) * 8 + z


def moved(value, target, places=PLACES):
    return lax.ppermute(value, ALL, [(number(*p), number(*target(*p))) for p in places])


def up(value):
    return moved(value, lambda y, x, c, z: (y, x, c, (z + 1) % 8))


def down(value):
    return moved(value, lambda y, x, c, z: (y, x, c, (z + 7) % 8))


def spread(block, axis, count):
    return lax.all_to_all(jnp.broadcast_to(block[None], (count,) + block.shape), axis, 0, 0)


def add_up(pieces):
    arrived = lax.all_to_all(pieces.reshape(32, 2 * B, 128), ORB, 0, 0)
    total = arrived.astype(F32).sum(0) * (0.25 / B)

    def send(half):
        def target(y, x, c, z):
            row, col = TILES[y * 2 + c][half]
            orb = ((z + col) % 8) * 4 + x
            return orb // 8, orb // 2 % 4, orb % 2, (z + row) % 8

        return moved(total[half * B:(half + 1) * B], target)

    return jnp.concatenate([send(0), send(1)], axis=1).T


def body(three_centre, occ_blocks, virt_blocks, occ_list, virt_list, term_count):
    both = jnp.concatenate([occ_blocks[0], virt_blocks[0]], axis=1)
    own = order_rows(three_centre[0])
    column = spread(both, "z", 8)
    own, column = lax.optimization_barrier((own, column))
    below_first, above_first = up(own[0]), down(own[1])
    below_last, above_last = up(own[1]), down(own[0])
    far_below_first, far_above_first = up(below_first), down(above_first)

    held = [column]
    for n in range(1, 4):
        held.append(moved(column, lambda y, x, c, z: ((y + n) % 4, x, c, z)))
    held = jnp.concatenate(held, axis=0)
    chosen = choose(held, occ_list, virt_list)
    arrived = lax.all_to_all(chosen.reshape(8, 8, B, 2 * B), ("x", "c"), 0, 0)
    w1, w2 = term_weights(term_count, arrived)
    image = image_rows(own[0], own[1], w1, w2)

    image, below_last, above_last = lax.optimization_barrier((image, below_last, above_last))
    far_below_last, far_above_last = up(below_last), down(above_last)
    near = image_rows(below_last, above_last, w1, w2)
    above, below = [(2, 0), (3, 1)], [(4, 0), (5, 1)]
    columns = [own[0], own[1], above_last, above_first, below_first, below_last]
    sums = tiles(
        [image, near],
        columns,
        [
            ([(0, 0), (1, 1)], [(0, 0, (0, 0)), (0, 1, (0, 1))]),
            (above, [(0, 0, (1, 0)), (0, 1, (1, 1)), (1, 0, (3, 1))]),
            (below, [(0, 0, (2, 0)), (0, 1, (2, 1)), (1, 1, (4, 0))]),
        ],
    )
    early = [(0, 0), (0, 1), (1, 0), (1, 1), (3, 1), (2, 0), (2, 1), (4, 0)]
    given = [(place, side) for place in early for side in range(2)]
    sums, far_below_first, far_above_first = lax.optimization_barrier((sums, far_below_first, far_above_first))
    far = image_rows(far_below_first, far_above_first, w1, w2)
    far_above = [(0, 0, (3, 0)), (1, 0, (5, 1)), (2, 0, (7, 0))]
    far_below = [(0, 1, (4, 1)), (1, 1, (6, 0)), (2, 1, (7, 1))]
    sums = tiles(
        [image, near, far],
        columns[2:] + [far_above_first, far_below_first],
        [
            ([(0, 0), (1, 1)], [(2, 0, (5, 0))]),
            ([(2, 0), (3, 1)], [(2, 1, (6, 1))]),
            ([(4, 1)], far_above),
            ([(5, 0)], far_below),
        ],
        sums,
        given,
    )
    given = given + [((5, 0), 0), ((5, 0), 1), ((6, 1), 0), ((6, 1), 1)]
    given = given + [(place, 1) for _, _, place in far_above] + [(place, 0) for _, _, place in far_below]
    sums, far_above_last, far_below_last = lax.optimization_barrier((sums, far_above_last, far_below_last))
    sums = tiles(
        [image, near, far],
        [far_above_last, far_below_last],
        [([(0, 0)], far_above), ([(1, 1)], far_below)],
        sums,
        given,
    )
    return add_up(sums)


def solution(mesh):
    fine = Mesh(mesh.devices.reshape(4, 4, 2, 8), ALL)
    blocks = P(ALL, None, None)
    inputs = (P(ORB, "z", None), blocks, blocks, P(), P(), P())
    return jax.shard_map(body, mesh=fine, in_specs=inputs, out_specs=P("z", ORB), check_vma=False)
```
